512 devices in a mesh: tm: 32 (over x_hi, z), head: 16 (over x_lo, y, core).
Axes of the slice: x: 4 (x_hi: 2, x_lo: 2; x = x_hi * 2 + x_lo), y: 4, z: 16, core: 2. Of those that a mesh axis runs over, the one named last changes fastest.
Arguments:
- queries: bfloat16 [73728, 4096], P(('tm', 'head')), may hold values from -8 to 8
- keys: bfloat16 [73728, 4096], P(('tm', 'head')), may hold values from -8 to 8
- values: bfloat16 [73728, 4096], P(('tm', 'head')), may hold values from -6 to 6
- tile_list: int32 [192, 7], P('tm'), may hold values from 0 to 191, as said below
- tile_count: int32 [192], P('tm'), may hold values from 1 to 7
Outputs:
- attended: bfloat16 [73728, 4096], P(('tm', 'head'))
The draws below stay inside these ranges and needn't reach their ends.
Inputs may be any that keep to these rules, and one draw needn't show every extreme that they name: `tile_list`: row t lists distinct tiles of t's time slab (tiles t // 6 * 6 and on) and of the slabs just before and after it; the first slot is t itself; every slot holds such a tile, also past the count.
All inputs are finite; a program needn't handle non-finite values.
Results may differ from the reference program's by a relative error of at most 0.0046.
Values may be sent and summed in bfloat16 or wider, within the bound.
A program may use at most 64 MiB of HBM per device.

```python
import jax
import jax.numpy as jnp
from jax import lax

HD = 128
TILE = 384
TILES_SLAB = 6
MAXLIST = 7
HEADS = 32
TOKENS = 73728
N_TM = 32


def draw_queries(key, part):
    drawn = jax.random.normal(jax.random.fold_in(key, 1), (TOKENS, HEADS * HD), jnp.float32)
    drawn = jnp.clip(drawn, -8.0, 8.0)
    return drawn.astype(jnp.bfloat16)


def draw_keys(key, part):
    drawn = jax.random.normal(jax.random.fold_in(key, 2), (TOKENS, HEADS * HD), jnp.float32)
    drawn = jnp.clip(drawn, -8.0, 8.0)
    return drawn.astype(jnp.bfloat16)


def tile_choice(key):
    all_tiles = TILES_SLAB * N_TM
    window_tiles = 3 * TILES_SLAB
    own_tile = jnp.arange(all_tiles, dtype=jnp.int32)
    slab_index = own_tile // TILES_SLAB
    offsets = jnp.arange(window_tiles, dtype=jnp.int32)
    candidates = (slab_index[:, None] - 1) * TILES_SLAB + offsets[None, :]
    usable = (candidates >= 0) & (candidates < all_tiles)
    rank_draw = jax.random.randint(jax.random.fold_in(key, 21), (all_tiles, window_tiles), 0, 1000)
    priority = rank_draw * window_tiles + offsets[None, :]
    priority = jnp.where(candidates == own_tile[:, None], 1001 * window_tiles, priority)
    priority = jnp.where(usable, priority, -1)
    unused, picked = lax.top_k(priority, MAXLIST)
    listed = jnp.take_along_axis(candidates, picked, axis=1).astype(jnp.int32)
    counts = jax.random.randint(jax.random.fold_in(key, 22), (all_tiles,), 1, MAXLIST + 1)
    at_edge = (slab_index == 0) | (slab_index == N_TM - 1)
    counts = jnp.where(at_edge, (counts + 1) // 2, counts)
    forced = jax.random.randint(jax.random.fold_in(key, 23), (), TILES_SLAB, all_tiles - TILES_SLAB)
    counts = jnp.where(own_tile == forced, MAXLIST, counts)
    return (listed, counts.astype(jnp.int32))


def draw_tile_list(key, part):
    return tile_choice(key)[0]


def draw_tile_count(key, part):
    return tile_choice(key)[1]


def steps_of(rng, dims, pieces, smallest, high):
    loudness = 1.0
    for dim, blocks in pieces:
        draws = jax.random.uniform(jax.random.fold_in(jax.random.fold_in(rng, 6), dim), (blocks,), jnp.float32, smallest / len(pieces), high / len(pieces))
        loudness = loudness * jnp.repeat(jnp.exp(draws), dims[dim] // blocks).reshape((-1,) + (1,) * (len(dims) - 1 - dim))
    return loudness


def gaussian(rng, shape, deviation, limit, pieces=(), held_as=jnp.bfloat16):
    values = deviation * jax.random.normal(rng, shape, jnp.float32)
    if pieces:
        values = values * steps_of(rng, shape, pieces, -0.22, 0.18)
    return jnp.clip(values, -limit, limit).astype(held_as)


def setup_inputs(seed: int = 0) -> dict:
    splits = jax.random.split(jax.random.key(seed), 6)
    queries = draw_queries(jax.random.fold_in(splits[5], 71), 0)
    keys = draw_keys(jax.random.fold_in(splits[5], 71), 0)
    values = gaussian(splits[2], (TOKENS, HEADS * HD), 1.0, 6.0, ((0, 512),))
    tile_list = draw_tile_list(jax.random.fold_in(splits[5], 71), 0)
    tile_count = draw_tile_count(jax.random.fold_in(splits[5], 71), 0)
    return {"queries": queries, "keys": keys, "values": values, "tile_list": tile_list, "tile_count": tile_count}


def reference(queries, keys, values, tile_list, tile_count):
    all_tiles = tile_list.shape[0]
    row_width = queries.shape[1]
    head_total = row_width // HD
    query_four = queries.reshape(all_tiles, TILE, head_total, HD)
    key_four = keys.reshape(all_tiles, TILE, head_total, HD)
    value_four = values.reshape(all_tiles, TILE, head_total, HD)
    key_span = MAXLIST * TILE
    slot_tile = jnp.arange(key_span, dtype=jnp.int32) // TILE
    scaling = HD ** -0.5

    def per_tile(operands):
        query_tile, listed, live_count = operands
        key_block = jnp.take(key_four, listed, axis=0).reshape(key_span, head_total, HD)
        value_block = jnp.take(value_four, listed, axis=0).reshape(key_span, head_total, HD)
        scores = jnp.einsum("qhd,khd->hqk", query_tile.astype(jnp.float32), key_block.astype(jnp.float32)) * scaling
        live_slots = slot_tile < live_count
        scores = jnp.where(live_slots[None, None, :], scores, -jnp.inf)
        highest = jnp.max(scores, axis=-1, keepdims=True)
        raised = jnp.exp(scores - highest)
        totals = jnp.sum(raised, axis=-1)
        weights = lax.optimization_barrier(raised.astype(jnp.bfloat16)).astype(jnp.float32)
        accumulated = jnp.einsum("hqk,khd->qhd", weights, value_block.astype(jnp.float32))
        return (accumulated / jnp.transpose(totals)[:, :, None]).astype(jnp.bfloat16)

    output = lax.map(per_tile, (query_four, tile_list, tile_count))
    return output.reshape(-1, row_width)
```

```python
import functools

import jax
import jax.numpy as jnp
from jax import lax
from jax.experimental import pallas as pl
from jax.experimental.pallas import tpu as pltpu
from jax.sharding import PartitionSpec as P

HD = 128
TILE = 384
BLOCK = 48
PER_TILE = TILE // BLOCK
LOG2E = 1.4426950408889634
NT = (((1,), (1,)), ((), ()))
MESH = pl.DeviceIdType.MESH


def tile_of(ref, first_block):
    return ref[pl.ds(first_block, PER_TILE)].reshape(TILE, HD)


def tile_attention(query, key_ref, value_ref, starts, biases, scale, score_ref):
    slots = len(starts)
    highest = None
    for s in range(slots):
        key_tile = tile_of(key_ref, starts[s])
        score = lax.dot_general(query, key_tile, NT, preferred_element_type=jnp.float32)
        score_ref[:, s * TILE : (s + 1) * TILE] = score
    for s in range(slots):
        score = score_ref[:, s * TILE : (s + 1) * TILE]
        top = jnp.max(score, axis=1, keepdims=True) * scale + biases[s]
        highest = top if highest is None else jnp.maximum(highest, top)
    total = jnp.zeros((TILE, 1), jnp.float32)
    summed = jnp.zeros((TILE, HD), jnp.float32)
    for s in range(slots):
        score = score_ref[:, s * TILE : (s + 1) * TILE]
        raised = jnp.exp2(score * scale - (highest - biases[s]))
        total += jnp.sum(raised, axis=1, keepdims=True)
        value_tile = tile_of(value_ref, starts[s])
        summed += jnp.dot(
            raised.astype(jnp.bfloat16), value_tile, preferred_element_type=jnp.float32
        )
    return summed * (1.0 / total)


def kernel(
    n_tm, half, group, tiles, slots,
    list_ref, count_ref, q_ref, k_ref, v_ref, o_ref,
    qa, ka, va, qb, kb, vb, oa, ob, score_ref,
    own_sem, send_sem, recv_sem, zsend_sem, zrecv_sem, osend_sem, orecv_sem, oown_sem,
):
    tok = q_ref.shape[0]
    slab = group * tok
    tm = lax.axis_index("tm")
    me = lax.axis_index("head")
    mirror = (group // 2) * (tm // half)
    mine = lax.rem(me + mirror, group)
    up_tm = lax.rem(tm + 1, n_tm)
    down_tm = lax.rem(tm + n_tm - 1, n_tm)
    up = (up_tm, lax.rem(mine + (group // 2) * (up_tm // half), group))
    down = (down_tm, lax.rem(mine + (group // 2) * (down_tm // half), group))

    sources = (k_ref, v_ref, q_ref)
    parts = {
        "ka": (ka, k_ref, 0, slab, 0),
        "va": (va, v_ref, 0, slab, 1),
        "kb": (kb, k_ref, 1, slab, 2),
        "vb": (vb, v_ref, 1, slab, 3),
        "qa": (qa, q_ref, 0, 0, 4),
        "qb": (qb, q_ref, 1, 0, 5),
    }

    def columns(owner, head):
        return pl.ds(pl.multiple_of(owner * (2 * HD) + head * HD, HD), HD)

    def rows(first, device):
        return pl.ds(first + device * tok, tok)

    def own_copy(name):
        buf, src, head, first, t = parts[name]
        return pltpu.make_async_copy(
            src.at[:, :, columns(mine, head)], buf.at[rows(first, me)], own_sem.at[t]
        )

    def spread(name):
        buf, src, head, first, t = parts[name]

        def step(d, carry):
            peer = lax.rem(me + d, group)
            pltpu.make_async_remote_copy(
                src_ref=src.at[:, :, columns(lax.rem(peer + mirror, group), head)],
                dst_ref=buf.at[rows(first, me)],
                send_sem=send_sem.at[t],
                recv_sem=recv_sem.at[t, me],
                device_id=(tm, peer),
                device_id_type=MESH,
            ).start()
            return carry

        lax.fori_loop(1, group, step, 0)

    def arrived(name, source):
        buf, _, _, first, t = parts[name]
        pltpu.make_async_copy(
            buf.at[rows(first, source)], buf.at[rows(first, source)], recv_sem.at[t, source]
        ).wait()

    def to_halo(name, source):
        buf, _, _, first, t = parts[name]
        for way, device, landing in ((0, up, 0), (1, down, 2 * slab)):
            pltpu.make_async_remote_copy(
                src_ref=buf.at[rows(first, source)],
                dst_ref=buf.at[rows(landing, source)],
                send_sem=zsend_sem.at[t, way],
                recv_sem=zrecv_sem.at[t, way],
                device_id=device,
                device_id_type=MESH,
            ).start()

    def forward(name):
        own_copy(name).wait()
        to_halo(name, me)

        def step(d, carry):
            source = lax.rem(me + group - d, group)
            arrived(name, source)
            to_halo(name, source)
            return carry

        lax.fori_loop(1, group, step, 0)

    def gather(name):
        own_copy(name).wait()

        def step(d, carry):
            arrived(name, lax.rem(me + group - d, group))
            return carry

        lax.fori_loop(1, group, step, 0)

    def halo_wait(name, sems):
        buf, _, _, _, t = parts[name]
        for way in range(2):
            whole = buf.at[pl.ds(0, slab)]
            pltpu.make_async_copy(whole, whole, sems.at[t, way]).wait()

    def return_rows(out_buf, head, device):
        @pl.when(device != me)
        def _():
            pltpu.make_async_remote_copy(
                src_ref=out_buf.at[rows(0, device)],
                dst_ref=o_ref.at[:, :, columns(mine, head)],
                send_sem=osend_sem.at[head],
                recv_sem=orecv_sem.at[head],
                device_id=(tm, device),
                device_id_type=MESH,
            ).start()

        @pl.when(device == me)
        def _():
            pltpu.make_async_copy(
                out_buf.at[rows(0, device)], o_ref.at[:, :, columns(mine, head)], oown_sem.at[head]
            ).start()

    scale = HD ** (-0.5) * LOG2E

    def attend(names, out_buf, head, between=None):
        query_buf, key_buf, value_buf = (parts[n][0] for n in names)

        def step(i, carry):
            if between is not None:
                pl.when(i == tiles // 2)(between)
            starts = [
                jnp.clip(list_ref[i, s] - (tm - 1) * tiles, 0, 3 * tiles - 1) * PER_TILE
                for s in range(slots)
            ]
            count = count_ref[i]
            biases = [
                (jnp.minimum(count - s, 1) - 1).astype(jnp.float32) * 1e30 for s in range(slots)
            ]
            result = tile_attention(
                tile_of(query_buf, i * PER_TILE), key_buf, value_buf, starts, biases, scale, score_ref
            )
            out_buf[pl.ds(i * PER_TILE, PER_TILE)] = result.astype(out_buf.dtype).reshape(
                PER_TILE, BLOCK, HD
            )

            def send(device, carry):
                return_rows(out_buf, head, device)
                return carry

            lax.fori_loop((i * PER_TILE) // tok, ((i + 1) * PER_TILE) // tok, send, 0)
            return carry

        lax.fori_loop(0, tiles, step, 0)

    order = ("ka", "va", "kb", "qa", "vb", "qb")
    for name in order:
        own_copy(name).start()

    barrier = pltpu.get_barrier_semaphore()

    def greet(d, carry):
        pl.semaphore_signal(
            barrier, inc=1, device_id=(tm, lax.rem(me + d, group)), device_id_type=MESH
        )
        return carry

    lax.fori_loop(1, group, greet, 0)
    for device in (up, down):
        pl.semaphore_signal(barrier, inc=1, device_id=device, device_id_type=MESH)
    pl.semaphore_wait(barrier, group + 1)

    for name in order:
        spread(name)
    forward("ka")
    forward("va")
    forward("kb")
    gather("qa")
    for name in ("ka", "va"):
        halo_wait(name, zrecv_sem)
    attend(("qa", "ka", "va"), oa, 0, lambda: forward("vb"))
    gather("qb")
    for name in ("kb", "vb"):
        halo_wait(name, zrecv_sem)
    attend(("qb", "kb", "vb"), ob, 1)

    for name in order:
        buf, _, _, first, t = parts[name]
        sent = buf.at[pl.ds(first, (group - 1) * tok)]
        pltpu.make_async_copy(sent, sent, send_sem.at[t]).wait()
    for name in ("ka", "va", "kb", "vb"):
        halo_wait(name, zsend_sem)
    for head, out_buf in enumerate((oa, ob)):
        others = out_buf.at[pl.ds(0, (group - 1) * tok)]
        pltpu.make_async_copy(others, others, osend_sem.at[head]).wait()
        pltpu.make_async_copy(others, others, orecv_sem.at[head]).wait()
        pltpu.make_async_copy(
            out_buf.at[rows(0, me)], o_ref.at[:, :, columns(mine, head)], oown_sem.at[head]
        ).wait()


def shards(queries, keys, values, tile_list, tile_count):
    n_tm, group = lax.axis_size("tm"), lax.axis_size("head")
    rows, width = queries.shape
    tok = rows // BLOCK
    slab = group * tok
    tiles, slots = tile_list.shape
    smem = pl.BlockSpec(memory_space=pltpu.SMEM)
    anywhere = pl.BlockSpec(memory_space=pl.ANY)
    narrow = pltpu.VMEM((slab, BLOCK, HD), jnp.bfloat16)
    wide = pltpu.VMEM((3 * slab, BLOCK, HD), jnp.bfloat16)
    dma = pltpu.SemaphoreType.DMA
    out = pl.pallas_call(
        functools.partial(kernel, n_tm, n_tm // 2, group, tiles, slots),
        out_shape=jax.ShapeDtypeStruct((tok, BLOCK, width), queries.dtype),
        in_specs=[smem, smem, anywhere, anywhere, anywhere],
        out_specs=anywhere,
        scratch_shapes=[
            narrow, wide, wide, narrow, wide, wide, narrow, narrow,
            pltpu.VMEM((TILE, slots * TILE), jnp.float32),
            dma((6,)), dma((6,)), dma((6, group)), dma((4, 2)), dma((4, 2)),
            dma((2,)), dma((2,)), dma((2,)),
        ],
        compiler_params=pltpu.CompilerParams(
            collective_id=0, has_side_effects=True, vmem_limit_bytes=48 * 2**20
        ),
    )(tile_list, tile_count, *(x.reshape(tok, BLOCK, width) for x in (queries, keys, values)))
    return out.reshape(rows, width)


def solution(mesh):
    by_token, by_tile = P(("tm", "head"), None), P("tm", None)
    return jax.shard_map(
        shards,
        mesh=mesh,
        in_specs=(by_token, by_token, by_token, by_tile, P("tm")),
        out_specs=by_token,
        check_vma=False,
    )
```

```python
import functools

import jax
import jax.numpy as jnp
from jax import lax
from jax.experimental import pallas as pl
from jax.experimental.pallas import tpu as pltpu
from jax.sharding import PartitionSpec as P

HD = 128
TILE = 384
BLOCK = 48
PER_TILE = TILE // BLOCK
LOG2E = 1.4426950408889634
NT = (((1,), (1,)), ((), ()))
MESH = pl.DeviceIdType.MESH


def tile_of(ref, first_block):
    return ref[pl.ds(first_block, PER_TILE)].reshape(TILE, HD)


def score_tiles(query, key_ref, starts, biases, scale, score_ref):
    highest = None
    for s, start in enumerate(starts):
        key_tile = tile_of(key_ref, start)
        score_ref[:, s * TILE : (s + 1) * TILE] = lax.dot_general(
            query, key_tile, NT, preferred_element_type=jnp.float32
        )
    for s, bias in enumerate(biases):
        score = score_ref[:, s * TILE : (s + 1) * TILE]
        top = jnp.max(score, axis=1, keepdims=True) * scale + bias
        highest = top if highest is None else jnp.maximum(highest, top)
    return highest


def raised_tile(score_ref, s, scale, highest, bias):
    return jnp.exp2(score_ref[:, s * TILE : (s + 1) * TILE] * scale - (highest - bias))


def tile_attention(query, key_ref, value_ref, starts, biases, scale, score_ref):
    highest = score_tiles(query, key_ref, starts, biases, scale, score_ref)
    total = jnp.zeros((TILE, 1), jnp.float32)
    summed = jnp.zeros((TILE, HD), jnp.float32)
    for s, start in enumerate(starts):
        raised = raised_tile(score_ref, s, scale, highest, biases[s])
        total += jnp.sum(raised, axis=1, keepdims=True)
        summed += jnp.dot(
            raised.astype(jnp.bfloat16),
            tile_of(value_ref, start),
            preferred_element_type=jnp.float32,
        )
    return summed * (1.0 / total)


def tile_weights(query, key_ref, starts, biases, scale, score_ref, weight_ref, i):
    highest = score_tiles(query, key_ref, starts, biases, scale, score_ref)
    total = jnp.zeros((TILE, 1), jnp.float32)
    for s, bias in enumerate(biases):
        raised = raised_tile(score_ref, s, scale, highest, bias)
        total += jnp.sum(raised, axis=1, keepdims=True)
        weight_ref[i, :, s * TILE : (s + 1) * TILE] = raised.astype(jnp.bfloat16)
    return 1.0 / total


def weighted_sum(value_ref, starts, weight_ref, i):
    summed = jnp.zeros((TILE, HD), jnp.float32)
    for s, start in enumerate(starts):
        summed += jnp.dot(
            weight_ref[i, :, s * TILE : (s + 1) * TILE],
            tile_of(value_ref, start),
            preferred_element_type=jnp.float32,
        )
    return summed


def kernel(
    n_tm, half, group, tiles, slots,
    list_ref, count_ref, q_ref, k_ref, v_ref, o_ref,
    qa, ka, va, qb, kb, vb, oa, ob, score_ref, weight_ref, inverse_ref,
    own_sem, send_sem, recv_sem, zsend_sem, zrecv_sem, osend_sem, orecv_sem, oown_sem,
):
    tok = q_ref.shape[0]
    slab = group * tok
    tm = lax.axis_index("tm")
    me = lax.axis_index("head")
    mirror = (group // 2) * (tm // half)
    mine = lax.rem(me + mirror, group)
    up_tm = lax.rem(tm + 1, n_tm)
    down_tm = lax.rem(tm + n_tm - 1, n_tm)
    up = (up_tm, lax.rem(mine + (group // 2) * (up_tm // half), group))
    down = (down_tm, lax.rem(mine + (group // 2) * (down_tm // half), group))

    sources = (k_ref, v_ref, q_ref)
    parts = {
        "ka": (ka, k_ref, 0, slab, 0),
        "va": (va, v_ref, 0, slab, 1),
        "kb": (kb, k_ref, 1, slab, 2),
        "vb": (vb, v_ref, 1, slab, 3),
        "qa": (qa, q_ref, 0, 0, 4),
        "qb": (qb, q_ref, 1, 0, 5),
    }

    def columns(owner, head):
        return pl.ds(pl.multiple_of(owner * (2 * HD) + head * HD, HD), HD)

    def rows(first, device):
        return pl.ds(first + device * tok, tok)

    def own_copy(name):
        buf, src, head, first, t = parts[name]
        return pltpu.make_async_copy(
            src.at[:, :, columns(mine, head)], buf.at[rows(first, me)], own_sem.at[t]
        )

    def spread(name):
        buf, src, head, first, t = parts[name]

        def step(d, carry):
            peer = lax.rem(me + d, group)
            pltpu.make_async_remote_copy(
                src_ref=src.at[:, :, columns(lax.rem(peer + mirror, group), head)],
                dst_ref=buf.at[rows(first, me)],
                send_sem=send_sem.at[t],
                recv_sem=recv_sem.at[t, me],
                device_id=(tm, peer),
                device_id_type=MESH,
            ).start()
            return carry

        lax.fori_loop(1, group, step, 0)

    def arrived(name, source):
        buf, _, _, first, t = parts[name]
        pltpu.make_async_copy(
            buf.at[rows(first, source)], buf.at[rows(first, source)], recv_sem.at[t, source]
        ).wait()

    def to_halo(name, source):
        buf, _, _, first, t = parts[name]
        for way, device, landing in ((0, up, 0), (1, down, 2 * slab)):
            pltpu.make_async_remote_copy(
                src_ref=buf.at[rows(first, source)],
                dst_ref=buf.at[rows(landing, source)],
                send_sem=zsend_sem.at[t, way],
                recv_sem=zrecv_sem.at[t, way],
                device_id=device,
                device_id_type=MESH,
            ).start()

    def forward(name):
        def step(d, carry):
            source = lax.rem(me + group - d, group)
            arrived(name, source)
            to_halo(name, source)
            return carry

        lax.fori_loop(1, group, step, 0)

    def gather(name):
        own_copy(name).wait()

        def step(d, carry):
            arrived(name, lax.rem(me + group - d, group))
            return carry

        lax.fori_loop(1, group, step, 0)

    def halo_wait(name, sems):
        buf, _, _, _, t = parts[name]
        for way in range(2):
            whole = buf.at[pl.ds(0, slab)]
            pltpu.make_async_copy(whole, whole, sems.at[t, way]).wait()

    def return_rows(out_buf, head, device):
        @pl.when(device != me)
        def _():
            pltpu.make_async_remote_copy(
                src_ref=out_buf.at[rows(0, device)],
                dst_ref=o_ref.at[:, :, columns(mine, head)],
                send_sem=osend_sem.at[head],
                recv_sem=orecv_sem.at[head],
                device_id=(tm, device),
                device_id_type=MESH,
            ).start()

        @pl.when(device == me)
        def _():
            pltpu.make_async_copy(
                out_buf.at[rows(0, device)], o_ref.at[:, :, columns(mine, head)], oown_sem.at[head]
            ).start()

    scale = HD ** (-0.5) * LOG2E

    def starts_of(i):
        return [
            jnp.clip(list_ref[i, s] - (tm - 1) * tiles, 0, 3 * tiles - 1) * PER_TILE
            for s in range(slots)
        ]

    def biases_of(i):
        return [
            (jnp.minimum(count_ref[i] - s, 1) - 1).astype(jnp.float32) * 1e30
            for s in range(slots)
        ]

    def finish(out_buf, head, i, result):
        out_buf[pl.ds(i * PER_TILE, PER_TILE)] = result.astype(out_buf.dtype).reshape(
            PER_TILE, BLOCK, HD
        )

        def send(device, carry):
            return_rows(out_buf, head, device)
            return carry

        lax.fori_loop((i * PER_TILE) // tok, ((i + 1) * PER_TILE) // tok, send, 0)

    def first_head(i, carry):
        pl.when(i == tiles // 2)(lambda: forward("vb"))
        result = tile_attention(
            tile_of(qa, i * PER_TILE), ka, va, starts_of(i), biases_of(i), scale, score_ref
        )
        finish(oa, 0, i, result)
        return carry

    def second_weights(i, carry):
        inverse_ref[i] = tile_weights(
            tile_of(qb, i * PER_TILE), kb, starts_of(i), biases_of(i), scale, score_ref,
            weight_ref, i,
        )
        return carry

    def second_head(i, carry):
        result = weighted_sum(vb, starts_of(i), weight_ref, i) * inverse_ref[i]
        finish(ob, 1, i, result)
        return carry

    order = ("ka", "va", "kb", "qa", "vb", "qb")
    for name in order:
        own_copy(name).start()

    barrier = pltpu.get_barrier_semaphore()

    def greet(d, carry):
        pl.semaphore_signal(
            barrier, inc=1, device_id=(tm, lax.rem(me + d, group)), device_id_type=MESH
        )
        return carry

    lax.fori_loop(1, group, greet, 0)
    for device in (up, down):
        pl.semaphore_signal(barrier, inc=1, device_id=device, device_id_type=MESH)
    pl.semaphore_wait(barrier, group + 1)

    for name in ("ka", "va", "kb", "vb"):
        own_copy(name).wait()
        to_halo(name, me)
    for name in order:
        spread(name)
    forward("ka")
    forward("va")
    forward("kb")
    gather("qa")
    halo_wait("ka", zrecv_sem)
    halo_wait("va", zrecv_sem)
    lax.fori_loop(0, tiles, first_head, 0)
    gather("qb")
    halo_wait("kb", zrecv_sem)
    lax.fori_loop(0, tiles, second_weights, 0)
    halo_wait("vb", zrecv_sem)
    lax.fori_loop(0, tiles, second_head, 0)

    for name in order:
        buf, _, _, first, t = parts[name]
        sent = buf.at[pl.ds(first, (group - 1) * tok)]
        pltpu.make_async_copy(sent, sent, send_sem.at[t]).wait()
    for name in ("ka", "va", "kb", "vb"):
        halo_wait(name, zsend_sem)
    for head, out_buf in enumerate((oa, ob)):
        others = out_buf.at[pl.ds(0, (group - 1) * tok)]
        pltpu.make_async_copy(others, others, osend_sem.at[head]).wait()
        pltpu.make_async_copy(others, others, orecv_sem.at[head]).wait()
        pltpu.make_async_copy(
            out_buf.at[rows(0, me)], o_ref.at[:, :, columns(mine, head)], oown_sem.at[head]
        ).wait()


def shards(queries, keys, values, tile_list, tile_count):
    n_tm, group = lax.axis_size("tm"), lax.axis_size("head")
    rows, width = queries.shape
    tok = rows // BLOCK
    slab = group * tok
    tiles, slots = tile_list.shape
    smem = pl.BlockSpec(memory_space=pltpu.SMEM)
    anywhere = pl.BlockSpec(memory_space=pl.ANY)
    narrow = pltpu.VMEM((slab, BLOCK, HD), jnp.bfloat16)
    wide = pltpu.VMEM((3 * slab, BLOCK, HD), jnp.bfloat16)
    dma = pltpu.SemaphoreType.DMA
    out = pl.pallas_call(
        functools.partial(kernel, n_tm, n_tm // 2, group, tiles, slots),
        out_shape=jax.ShapeDtypeStruct((tok, BLOCK, width), queries.dtype),
        in_specs=[smem, smem, anywhere, anywhere, anywhere],
        out_specs=anywhere,
        scratch_shapes=[
            narrow, wide, wide, narrow, wide, wide, narrow, narrow,
            pltpu.VMEM((TILE, slots * TILE), jnp.float32),
            pltpu.VMEM((tiles, TILE, slots * TILE), jnp.bfloat16),
            pltpu.VMEM((tiles, TILE, 1), jnp.float32),
            dma((6,)), dma((6,)), dma((6, group)), dma((4, 2)), dma((4, 2)),
            dma((2,)), dma((2,)), dma((2,)),
        ],
        compiler_params=pltpu.CompilerParams(
            collective_id=0, has_side_effects=True, vmem_limit_bytes=60 * 2**20
        ),
    )(tile_list, tile_count, *(x.reshape(tok, BLOCK, width) for x in (queries, keys, values)))
    return out.reshape(rows, width)


def solution(mesh):
    by_token, by_tile = P(("tm", "head"), None), P("tm", None)
    return jax.shard_map(
        shards,
        mesh=mesh,
        in_specs=(by_token, by_token, by_token, by_tile, P("tm")),
        out_specs=by_token,
        check_vma=False,
    )
```

```python
import functools

import jax
import jax.numpy as jnp
from jax import lax
from jax.experimental import pallas as pl
from jax.experimental.pallas import tpu as pltpu
from jax.sharding import PartitionSpec as P

HD = 128
TILE = 384
BLOCK = 48
PER_TILE = TILE // BLOCK
LOG2E = 1.4426950408889634
NT = (((1,), (1,)), ((), ()))
MESH = pl.DeviceIdType.MESH


def tile_of(ref, first_block):
    return ref[pl.ds(first_block, PER_TILE)].reshape(TILE, HD)


def score_tiles(query, key_ref, starts, biases, scale, score_ref):
    highest = None
    for s, start in enumerate(starts):
        key_tile = tile_of(key_ref, start)
        score_ref[:, s * TILE : (s + 1) * TILE] = lax.dot_general(
            query, key_tile, NT, preferred_element_type=jnp.float32
        )
    for s, bias in enumerate(biases):
        score = score_ref[:, s * TILE : (s + 1) * TILE]
        top = jnp.max(score, axis=1, keepdims=True) * scale + bias
        highest = top if highest is None else jnp.maximum(highest, top)
    return highest


def raised_tile(score_ref, s, scale, highest, bias):
    return jnp.exp2(score_ref[:, s * TILE : (s + 1) * TILE] * scale - (highest - bias))


def tile_attention(query, key_ref, value_ref, starts, biases, scale, score_ref):
    highest = score_tiles(query, key_ref, starts, biases, scale, score_ref)
    total = jnp.zeros((TILE, 1), jnp.float32)
    summed = jnp.zeros((TILE, HD), jnp.float32)
    for s, start in enumerate(starts):
        raised = raised_tile(score_ref, s, scale, highest, biases[s])
        total += jnp.sum(raised, axis=1, keepdims=True)
        summed += jnp.dot(
            raised.astype(jnp.bfloat16),
            tile_of(value_ref, start),
            preferred_element_type=jnp.float32,
        )
    return summed * (1.0 / total)


def tile_weights(query, key_ref, starts, biases, scale, score_ref, weight_ref, i):
    highest = score_tiles(query, key_ref, starts, biases, scale, score_ref)
    total = jnp.zeros((TILE, 1), jnp.float32)
    for s, bias in enumerate(biases):
        raised = raised_tile(score_ref, s, scale, highest, bias)
        total += jnp.sum(raised, axis=1, keepdims=True)
        weight_ref[i, :, s * TILE : (s + 1) * TILE] = raised.astype(jnp.bfloat16)
    return 1.0 / total


def weighted_sum(value_ref, starts, weight_ref, i):
    summed = jnp.zeros((TILE, HD), jnp.float32)
    for s, start in enumerate(starts):
        summed += jnp.dot(
            weight_ref[i, :, s * TILE : (s + 1) * TILE],
            tile_of(value_ref, start),
            preferred_element_type=jnp.float32,
        )
    return summed


def kernel(
    n_tm, half, group, tiles, slots,
    list_ref, count_ref, q_ref, k_ref, v_ref, o_ref,
    qa, ka, va, qb, kb, vb, oa, ob, score_ref, weight_ref, inverse_ref,
    own_sem, send_sem, recv_sem, zsend_sem, zrecv_sem, osend_sem, orecv_sem, oown_sem,
):
    tok = q_ref.shape[0]
    slab = group * tok
    tm = lax.axis_index("tm")
    me = lax.axis_index("head")
    mirror = (group // 2) * (tm // half)
    mine = lax.rem(me + mirror, group)
    up_tm = lax.rem(tm + 1, n_tm)
    down_tm = lax.rem(tm + n_tm - 1, n_tm)
    up = (up_tm, lax.rem(mine + (group // 2) * (up_tm // half), group))
    down = (down_tm, lax.rem(mine + (group // 2) * (down_tm // half), group))

    parts = {
        "ka": (ka, k_ref, 0, slab, 0),
        "va": (va, v_ref, 0, slab, 1),
        "kb": (kb, k_ref, 1, slab, 2),
        "vb": (vb, v_ref, 1, slab, 3),
        "qa": (qa, q_ref, 0, 0, 4),
        "qb": (qb, q_ref, 1, 0, 5),
    }

    def columns(owner, head):
        return pl.ds(pl.multiple_of(owner * (2 * HD) + head * HD, HD), HD)

    def rows(first, device):
        return pl.ds(first + device * tok, tok)

    def own_copy(name):
        buf, src, head, first, t = parts[name]
        return pltpu.make_async_copy(
            src.at[:, :, columns(mine, head)], buf.at[rows(first, me)], own_sem.at[t]
        )

    def spread(name):
        buf, src, head, first, t = parts[name]

        def step(d, carry):
            peer = lax.rem(me + d, group)
            pltpu.make_async_remote_copy(
                src_ref=src.at[:, :, columns(lax.rem(peer + mirror, group), head)],
                dst_ref=buf.at[rows(first, me)],
                send_sem=send_sem.at[t],
                recv_sem=recv_sem.at[t, me],
                device_id=(tm, peer),
                device_id_type=MESH,
            ).start()
            return carry

        lax.fori_loop(1, group, step, 0)

    def arrived(name, source):
        buf, _, _, first, t = parts[name]
        pltpu.make_async_copy(
            buf.at[rows(first, source)], buf.at[rows(first, source)], recv_sem.at[t, source]
        ).wait()

    def to_halo(name, source):
        buf, _, _, first, t = parts[name]
        for way, device, there, landing in (
            (0, up, tm < n_tm - 1, 0),
            (1, down, tm > 0, 2 * slab),
        ):

            @pl.when(there)
            def _(way=way, device=device, landing=landing):
                pltpu.make_async_remote_copy(
                    src_ref=buf.at[rows(first, source)],
                    dst_ref=buf.at[rows(landing, source)],
                    send_sem=zsend_sem.at[t, way],
                    recv_sem=zrecv_sem.at[t, way],
                    device_id=device,
                    device_id_type=MESH,
                ).start()

    def forward(name):
        def step(d, carry):
            source = lax.rem(me + group - d, group)
            arrived(name, source)
            to_halo(name, source)
            return carry

        lax.fori_loop(1, group, step, 0)

    def gather(name):
        own_copy(name).wait()

        def step(d, carry):
            arrived(name, lax.rem(me + group - d, group))
            return carry

        lax.fori_loop(1, group, step, 0)

    def halo_wait(name, sems, low_way):
        buf, _, _, _, t = parts[name]
        for way, there in ((low_way, tm > 0), (1 - low_way, tm < n_tm - 1)):

            @pl.when(there)
            def _(way=way):
                whole = buf.at[pl.ds(0, slab)]
                pltpu.make_async_copy(whole, whole, sems.at[t, way]).wait()

    def return_block(out_buf, head, block):
        device = block // tok
        src = out_buf.at[pl.ds(block, 1)]
        dst = o_ref.at[pl.ds(block - device * tok, 1), :, columns(mine, head)]

        @pl.when(device != me)
        def _():
            pltpu.make_async_remote_copy(
                src_ref=src,
                dst_ref=dst,
                send_sem=osend_sem.at[head],
                recv_sem=orecv_sem.at[head],
                device_id=(tm, device),
                device_id_type=MESH,
            ).start()

        @pl.when(device == me)
        def _():
            pltpu.make_async_copy(src, dst, oown_sem.at[head]).start()

    scale = HD ** (-0.5) * LOG2E

    def starts_of(i):
        return [
            jnp.clip(list_ref[i, s] - (tm - 1) * tiles, 0, 3 * tiles - 1) * PER_TILE
            for s in range(slots)
        ]

    def biases_of(i):
        return [
            (jnp.minimum(count_ref[i] - s, 1) - 1).astype(jnp.float32) * 1e30
            for s in range(slots)
        ]

    def finish(out_buf, head, i, result):
        out_buf[pl.ds(i * PER_TILE, PER_TILE)] = result.astype(out_buf.dtype).reshape(
            PER_TILE, BLOCK, HD
        )

        def send(b, carry):
            return_block(out_buf, head, i * PER_TILE + b)
            return carry

        lax.fori_loop(0, PER_TILE, send, 0)

    begin = (me * tiles) // group

    def first_head(j, carry):
        pl.when(j == tiles // 2)(lambda: forward("vb"))
        i = lax.rem(begin + j, tiles)
        result = tile_attention(
            tile_of(qa, i * PER_TILE), ka, va, starts_of(i), biases_of(i), scale, score_ref
        )
        finish(oa, 0, i, result)
        return carry

    def second_weights(i, carry):
        inverse_ref[i] = tile_weights(
            tile_of(qb, i * PER_TILE), kb, starts_of(i), biases_of(i), scale, score_ref,
            weight_ref, i,
        )
        return carry

    def second_head(j, carry):
        i = lax.rem(begin + j, tiles)
        result = weighted_sum(vb, starts_of(i), weight_ref, i) * inverse_ref[i]
        finish(ob, 1, i, result)
        return carry

    order = ("ka", "va", "kb", "qa", "vb", "qb")
    for name in order:
        own_copy(name).start()

    barrier = pltpu.get_barrier_semaphore()

    def greet(d, carry):
        pl.semaphore_signal(
            barrier, inc=1, device_id=(tm, lax.rem(me + d, group)), device_id_type=MESH
        )
        return carry

    lax.fori_loop(1, group, greet, 0)
    for device, there in ((up, tm < n_tm - 1), (down, tm > 0)):

        @pl.when(there)
        def _(device=device):
            pl.semaphore_signal(barrier, inc=1, device_id=device, device_id_type=MESH)

    beside = jnp.minimum(tm, 1) + jnp.minimum(n_tm - 1 - tm, 1)
    pl.semaphore_wait(barrier, group - 1 + beside)

    for name in ("ka", "va", "kb", "vb"):
        own_copy(name).wait()
        to_halo(name, me)
    for name in order:
        spread(name)
    forward("ka")
    forward("va")
    forward("kb")
    gather("qa")
    halo_wait("ka", zrecv_sem, 0)
    halo_wait("va", zrecv_sem, 0)
    lax.fori_loop(0, tiles, first_head, 0)
    gather("qb")
    halo_wait("kb", zrecv_sem, 0)
    lax.fori_loop(0, tiles, second_weights, 0)
    halo_wait("vb", zrecv_sem, 0)
    lax.fori_loop(0, tiles, second_head, 0)

    for name in order:
        buf, _, _, first, t = parts[name]
        sent = buf.at[pl.ds(first, (group - 1) * tok)]
        pltpu.make_async_copy(sent, sent, send_sem.at[t]).wait()
    for name in ("ka", "va", "kb", "vb"):
        halo_wait(name, zsend_sem, 1)
    for head, out_buf in enumerate((oa, ob)):
        others = out_buf.at[pl.ds(0, (group - 1) * tok)]
        pltpu.make_async_copy(others, others, osend_sem.at[head]).wait()
        pltpu.make_async_copy(others, others, orecv_sem.at[head]).wait()
        pltpu.make_async_copy(
            out_buf.at[rows(0, me)], o_ref.at[:, :, columns(mine, head)], oown_sem.at[head]
        ).wait()


def shards(queries, keys, values, tile_list, tile_count):
    n_tm, group = lax.axis_size("tm"), lax.axis_size("head")
    rows, width = queries.shape
    tok = rows // BLOCK
    slab = group * tok
    tiles, slots = tile_list.shape
    smem = pl.BlockSpec(memory_space=pltpu.SMEM)
    hbm = pl.BlockSpec(memory_space=pltpu.HBM)
    narrow = pltpu.VMEM((slab, BLOCK, HD), jnp.bfloat16)
    wide = pltpu.VMEM((3 * slab, BLOCK, HD), jnp.bfloat16)
    dma = pltpu.SemaphoreType.DMA
    out = pl.pallas_call(
        functools.partial(kernel, n_tm, n_tm // 2, group, tiles, slots),
        out_shape=pltpu.VMEM((tok, BLOCK, width), queries.dtype),
        in_specs=[smem, smem, hbm, hbm, hbm],
        out_specs=pl.BlockSpec(memory_space=pltpu.VMEM),
        scratch_shapes=[
            narrow, wide, wide, narrow, wide, wide, narrow, narrow,
            pltpu.VMEM((TILE, slots * TILE), jnp.float32),
            pltpu.VMEM((tiles, TILE, slots * TILE), jnp.bfloat16),
            pltpu.VMEM((tiles, TILE, 1), jnp.float32),
            dma((6,)), dma((6,)), dma((6, group)), dma((4, 2)), dma((4, 2)),
            dma((2,)), dma((2,)), dma((2,)),
        ],
        compiler_params=pltpu.CompilerParams(
            collective_id=0, has_side_effects=True, vmem_limit_bytes=60 * 2**20
        ),
    )(tile_list, tile_count, *(x.reshape(tok, BLOCK, width) for x in (queries, keys, values)))
    return out.reshape(rows, width)


def solution(mesh):
    by_token, by_tile = P(("tm", "head"), None), P("tm", None)
    return jax.shard_map(
        shards,
        mesh=mesh,
        in_specs=(by_token, by_token, by_token, by_tile, P("tm")),
        out_specs=by_token,
        check_vma=False,
    )
```
